32 devices in a mesh: section: 4 (over y, x), dp: 8 (over z, core).
Axes of the slice: x: 2, y: 2, z: 4, core: 2. Of those that a mesh axis runs over, the one named last changes fastest.
Arguments:
- ids: int32 [4, 1280, 32], P('section', 'dp'), may hold values from 0 to 49151, as said below
- masks: int32 [4, 1280, 32], P(None, 'dp'), may hold values 0 or 1
- labels: int32 [4, 1280], P(None, 'dp'), may hold values 0 or 1
- table: float32 [49152, 160], P('dp'), may hold values from -6 to 6
- table_first: float32 [49152, 160], P('dp'), may hold values from -3.8146973e-06 to 3.8146973e-06
- table_second: float32 [49152, 160], P('dp'), may hold values from 2.746582e-15 to 4.3945313e-14
- null_tokens: float32 [32, 160], replicated, may hold values from -6 to 6
- null_first: float32 [32, 160], replicated, may hold values from -4.5776367e-05 to 4.5776367e-05
- null_second: float32 [32, 160], replicated, may hold values from 3.90625e-13 to 6.25e-12
- w_up: float32 [2, 768, 1536], P(None, 'dp'), may hold values from -0.21875 to 0.21875
- up_first: float32 [2, 768, 1536], P(None, 'dp'), may hold values from -6.1035156e-05 to 6.1035156e-05
- up_second: float32 [2, 768, 1536], P(None, 'dp'), may hold values from 8.7890627e-13 to 1.40625e-11
- w_down: float32 [2, 1536, 2560], P(None, 'dp'), may hold values from -0.15625 to 0.15625
- down_first: float32 [2, 1536, 2560], P(None, 'dp'), may hold values from -6.1035156e-05 to 6.1035156e-05
- down_second: float32 [2, 1536, 2560], P(None, 'dp'), may hold values from 8.7890627e-13 to 1.40625e-11
- w_top: float32 [5120, 2048], P('dp'), may hold values from -0.078125 to 0.078125
- top_first: float32 [5120, 2048], P('dp'), may hold values from -0.00015258789 to 0.00015258789
- top_second: float32 [5120, 2048], P('dp'), may hold values from 4.785156e-12 to 7.65625e-11
- gains: float32 [2, 928], replicated, may hold values from 0.5 to 1.5
- gains_first: float32 [2, 928], replicated, may hold values from -0.00024414062 to 0.00024414062
- gains_second: float32 [2, 928], replicated, may hold values from 9.765625e-12 to 1.5625e-10
- biases: float32 [2, 5024], replicated, may hold values from -1.5 to 1.5
- biases_first: float32 [2, 5024], replicated, may hold values from -0.00012207031 to 0.00012207031
- biases_second: float32 [2, 5024], replicated, may hold values from 2.4414062e-12 to 3.90625e-11
- mixers: float32 [2, 1280], replicated, may hold values from -1 to 1
- mixers_first: float32 [2, 1280], replicated, may hold values from -0.00024414062 to 0.00024414062
- mixers_second: float32 [2, 1280], replicated, may hold values from 9.765625e-12 to 1.5625e-10
- top_bias: float32 [2048], replicated, may hold values from -1.5 to 1.5
- top_bias_first: float32 [2048], replicated, may hold values from -0.00015258789 to 0.00015258789
- top_bias_second: float32 [2048], replicated, may hold values from 4.785156e-12 to 7.65625e-11
- head: float32 [2049], replicated, may hold values from -1.5 to 1.5
- head_first: float32 [2049], replicated, may hold values from -0.0068359375 to 0.0068359375
- head_second: float32 [2049], replicated, may hold values from 8.789063e-09 to 1.40625e-07
Outputs:
- losses: float32 [4, 1280], P('section', 'dp')
- input_grad: bfloat16 [4, 1280, 32, 160], P('section', 'dp')
- table_new: float32 [49152, 160], P('dp')
- table_first_new: float32 [49152, 160], P('dp')
- table_second_new: float32 [49152, 160], P('dp')
- null_new: float32 [32, 160], replicated
- null_first_new: float32 [32, 160], replicated
- null_second_new: float32 [32, 160], replicated
- up_new: float32 [2, 768, 1536], P(None, 'dp')
- up_first_new: float32 [2, 768, 1536], P(None, 'dp')
- up_second_new: float32 [2, 768, 1536], P(None, 'dp')
- down_new: float32 [2, 1536, 2560], P(None, 'dp')
- down_first_new: float32 [2, 1536, 2560], P(None, 'dp')
- down_second_new: float32 [2, 1536, 2560], P(None, 'dp')
- top_new: float32 [5120, 2048], P('dp')
- top_first_new: float32 [5120, 2048], P('dp')
- top_second_new: float32 [5120, 2048], P('dp')
- gains_new: float32 [2, 928], replicated
- gains_first_new: float32 [2, 928], replicated
- gains_second_new: float32 [2, 928], replicated
- biases_new: float32 [2, 5024], replicated
- biases_first_new: float32 [2, 5024], replicated
- biases_second_new: float32 [2, 5024], replicated
- mixers_new: float32 [2, 1280], replicated
- mixers_first_new: float32 [2, 1280], replicated
- mixers_second_new: float32 [2, 1280], replicated
- top_bias_new: float32 [2048], replicated
- top_bias_first_new: float32 [2048], replicated
- top_bias_second_new: float32 [2048], replicated
- head_new: float32 [2049], replicated
- head_first_new: float32 [2049], replicated
- head_second_new: float32 [2049], replicated
The draws below stay inside these ranges and needn't reach their ends.
Inputs may be any that keep to these rules, and one draw needn't show every extreme that they name: Of the 5120 ids of one micro-batch on one index of dp (aligned blocks of ids), at most 1280 lie in the 6144 rows held by one index of dp, and in every block exactly 1280 do for some index.
All inputs are finite; a program needn't handle non-finite values. No bound on the sum of `masks` or of `labels` on one device may be relied on, other than what follows from the above.
Results may differ from the reference program's by a relative error of at most 0.022.
Values may be sent and summed in bfloat16 or wider, within the bound.
A program may use at most 640 MiB of HBM per device.

```python
import math
import jax
import jax.numpy as jnp
from jax import lax

D = 160
FEATS = 32
OUT_TOK = 16
LCB_TOK = 16
FM_RANK = 24
MLP_HID = 1536
TOP_HID = 2048
ROWS_DEV = 6144
EX = 160
STEP = 10
MICRO = 4
EXAMPLES = 1280
ROWS = 49152
MLP_IN = 768
N_DP = 8


def draw_ids(key, part):
    key = jax.random.fold_in(key, 11)
    block = EX * FEATS
    even = block // N_DP
    halves = N_DP // 2

    def one_group(sub):
        keys = jax.random.split(sub, 4)
        order = jax.random.permutation(keys[0], N_DP)
        delta = jax.random.randint(keys[1], (halves,), -(even // 2), even // 2 + 1)
        delta = delta.at[0].set(even)
        counts = jnp.zeros((N_DP,), jnp.int32)
        counts = counts.at[order[:halves]].set(even + delta)
        counts = counts.at[order[halves:]].set(even - delta)
        owners = jnp.repeat(jnp.arange(N_DP, dtype=jnp.int32), counts, total_repeat_length=block)
        owners = jax.random.permutation(keys[2], owners)
        local = jax.random.randint(keys[3], (block,), 0, ROWS_DEV)
        return owners * ROWS_DEV + local
    groups = jax.vmap(one_group)(jax.random.split(key, MICRO * N_DP))
    return groups.reshape(MICRO, N_DP * EX, FEATS).astype(jnp.int32)


def place_ends(result, key, low, high):
    place = [jax.random.randint(jax.random.fold_in(key, axis), (), 0, length) for axis, length in enumerate(result.shape)]
    widest = result.shape.index(max(result.shape))
    beside = place[:widest] + [(place[widest] + 1) % result.shape[widest]] + place[widest + 1:]
    return result.at[tuple(place)].set(low).at[tuple(beside)].set(high)


def block_levels(own_key, dims, shards, smallest, largest):
    gain = 1.0
    for position, parts in shards:
        steps = jax.random.uniform(jax.random.fold_in(jax.random.fold_in(own_key, 6), position), (parts,), jnp.float32, smallest / len(shards), largest / len(shards))
        gain = gain * jnp.repeat(jnp.exp(steps), dims[position] // parts).reshape((-1,) + (1,) * (len(dims) - 1 - position))
    return gain


def gaussian(key, shape, width, bound, pieces=(), held_as=jnp.bfloat16):
    result = width * jax.random.normal(key, shape, jnp.float32)
    if pieces:
        result = result * block_levels(key, shape, pieces, -0.22, 0.18)
    return jnp.clip(result, -bound, bound).astype(held_as)


def setup_inputs(seed: int = 0) -> dict:
    splits = jax.random.split(jax.random.key(seed), 34)
    ids = draw_ids(jax.random.fold_in(splits[33], 71), 0)
    masks = place_ends((jax.random.randint(splits[1], (MICRO, EXAMPLES, FEATS), 0, 4) < 3).astype(jnp.int32), jax.random.fold_in(splits[1], 1), 0, 1)
    labels = place_ends((jax.random.randint(splits[2], (MICRO, EXAMPLES), 0, 2) < 1).astype(jnp.int32), jax.random.fold_in(splits[2], 1), 0, 1)
    table = gaussian(splits[3], (ROWS, D), 1.0, 6.0, ((0, 8),), jnp.float32)
    table_first = gaussian(splits[4], (ROWS, D), (0.00132 / (MICRO * EXAMPLES)), 3.814697265625e-06, ((0, 8),), jnp.float32)
    table_second = jnp.clip(jnp.exp(math.log(4.394531274791967e-14) - 2.7725887 * jax.random.uniform(splits[5], (ROWS, D), jnp.float32) ** block_levels(splits[5], (ROWS, D), ((0, 8),), -0.2, 0.2)), 2.7465820467449794e-15, 4.394531274791967e-14)
    null_tokens = gaussian(splits[6], (FEATS, D), 1.0, 6.0, (), jnp.float32)
    null_first = gaussian(splits[7], (FEATS, D), (0.00022 * (MICRO * EXAMPLES) ** -0.5), 4.57763671875e-05, (), jnp.float32)
    null_second = jnp.clip(jnp.exp(jax.random.uniform(splits[8], (FEATS, D), jnp.float32, math.log(3.906250052154031e-13), math.log(6.25000008344645e-12))), 3.906250052154031e-13, 6.25000008344645e-12)
    w_up = gaussian(splits[9], (2, MLP_IN, MLP_HID), MLP_IN ** -0.5, 0.21875, ((1, 8),), jnp.float32)
    up_first = gaussian(splits[10], (2, MLP_IN, MLP_HID), (0.00033 * (MICRO * EXAMPLES) ** -0.5), 6.103515625e-05, ((1, 8),), jnp.float32)
    up_second = jnp.clip(jnp.exp(math.log(1.4062500296174729e-11) - 2.7725887 * jax.random.uniform(splits[11], (2, MLP_IN, MLP_HID), jnp.float32) ** block_levels(splits[11], (2, MLP_IN, MLP_HID), ((1, 8),), -0.2, 0.2)), 8.789062685109206e-13, 1.4062500296174729e-11)
    w_down = gaussian(splits[12], (2, MLP_HID, OUT_TOK * D), MLP_HID ** -0.5, 0.15625, ((1, 8),), jnp.float32)
    down_first = gaussian(splits[13], (2, MLP_HID, OUT_TOK * D), (0.00033 * (MICRO * EXAMPLES) ** -0.5), 6.103515625e-05, ((1, 8),), jnp.float32)
    down_second = jnp.clip(jnp.exp(math.log(1.4062500296174729e-11) - 2.7725887 * jax.random.uniform(splits[14], (2, MLP_HID, OUT_TOK * D), jnp.float32) ** block_levels(splits[14], (2, MLP_HID, OUT_TOK * D), ((1, 8),), -0.2, 0.2)), 8.789062685109206e-13, 1.4062500296174729e-11)
    w_top = gaussian(splits[15], (FEATS * D, TOP_HID), (FEATS * D) ** -0.5, 0.078125, ((0, 8),), jnp.float32)
    top_first = gaussian(splits[16], (FEATS * D, TOP_HID), (0.00077 * (MICRO * EXAMPLES) ** -0.5), 0.00015258789, ((0, 8),), jnp.float32)
    top_second = jnp.clip(jnp.exp(math.log(7.656249939591575e-11) - 2.7725887 * jax.random.uniform(splits[17], (FEATS * D, TOP_HID), jnp.float32) ** block_levels(splits[17], (FEATS * D, TOP_HID), ((0, 8),), -0.2, 0.2)), 4.7851562122447344e-12, 7.656249939591575e-11)
    gains = jnp.clip(1.0 + 0.1 * jax.random.normal(splits[18], (2, MLP_IN + D), jnp.float32), 0.5, 1.5)
    gains_first = gaussian(splits[19], (2, MLP_IN + D), (0.0011 * (MICRO * EXAMPLES) ** -0.5), 0.00024414062, (), jnp.float32)
    gains_second = jnp.clip(jnp.exp(jax.random.uniform(splits[20], (2, MLP_IN + D), jnp.float32, math.log(9.765624940649698e-12), math.log(1.5624999905039516e-10))), 9.765624940649698e-12, 1.5624999905039516e-10)
    biases = gaussian(splits[21], (2, MLP_IN + MLP_HID + OUT_TOK * D + D), 0.1, 1.5, (), jnp.float32)
    biases_first = gaussian(splits[22], (2, MLP_IN + MLP_HID + OUT_TOK * D + D), (0.00055 * (MICRO * EXAMPLES) ** -0.5), 0.00012207031, (), jnp.float32)
    biases_second = jnp.clip(jnp.exp(jax.random.uniform(splits[23], (2, MLP_IN + MLP_HID + OUT_TOK * D + D), jnp.float32, math.log(2.4414062351624244e-12), math.log(3.906249976259879e-11))), 2.4414062351624244e-12, 3.906249976259879e-11)
    mixers = gaussian(splits[24], (2, MLP_IN + LCB_TOK * FEATS), FEATS ** -0.5, 1.0, (), jnp.float32)
    mixers_first = gaussian(splits[25], (2, MLP_IN + LCB_TOK * FEATS), (0.0011 * (MICRO * EXAMPLES) ** -0.5), 0.00024414062, (), jnp.float32)
    mixers_second = jnp.clip(jnp.exp(jax.random.uniform(splits[26], (2, MLP_IN + LCB_TOK * FEATS), jnp.float32, math.log(9.765624940649698e-12), math.log(1.5624999905039516e-10))), 9.765624940649698e-12, 1.5624999905039516e-10)
    top_bias = gaussian(splits[27], (TOP_HID,), 0.1, 1.5, (), jnp.float32)
    top_bias_first = gaussian(splits[28], (TOP_HID,), (0.00077 * (MICRO * EXAMPLES) ** -0.5), 0.00015258789, (), jnp.float32)
    top_bias_second = jnp.clip(jnp.exp(jax.random.uniform(splits[29], (TOP_HID,), jnp.float32, math.log(4.7851562122447344e-12), math.log(7.656249939591575e-11))), 4.7851562122447344e-12, 7.656249939591575e-11)
    head = gaussian(splits[30], (TOP_HID + 1,), 0.1, 1.5, (), jnp.float32)
    head_first = gaussian(splits[31], (TOP_HID + 1,), (0.033 * (MICRO * EXAMPLES) ** -0.5), 0.0068359375, (), jnp.float32)
    head_second = jnp.clip(jnp.exp(jax.random.uniform(splits[32], (TOP_HID + 1,), jnp.float32, math.log(8.789062810876658e-09), math.log(1.4062500497402652e-07))), 8.789062810876658e-09, 1.4062500497402652e-07)
    return {"ids": ids, "masks": masks, "labels": labels, "table": table, "table_first": table_first, "table_second": table_second, "null_tokens": null_tokens, "null_first": null_first, "null_second": null_second, "w_up": w_up, "up_first": up_first, "up_second": up_second, "w_down": w_down, "down_first": down_first, "down_second": down_second, "w_top": w_top, "top_first": top_first, "top_second": top_second, "gains": gains, "gains_first": gains_first, "gains_second": gains_second, "biases": biases, "biases_first": biases_first, "biases_second": biases_second, "mixers": mixers, "mixers_first": mixers_first, "mixers_second": mixers_second, "top_bias": top_bias, "top_bias_first": top_bias_first, "top_bias_second": top_bias_second, "head": head, "head_first": head_first, "head_second": head_second}


@jax.custom_vjp
def low(v):
    return lax.optimization_barrier(v.astype(jnp.bfloat16)).astype(jnp.float32)

@jax.custom_vjp
def low_back(v):
    return v

def low_keep(v):
    return (low(v), None)

def low_pass(kept, grad):
    return (grad,)

def back_keep(v):
    return (v, None)

def back_low(kept, grad):
    return (low(grad),)
low.defvjp(low_keep, low_pass)
low_back.defvjp(back_keep, back_low)
beta_one = 0.9
beta_two = 0.999
adam_eps = 1e-08
norm_eps = 1e-05
highest = lax.Precision.HIGHEST

def layer_norm(values, scales, offsets):
    center = lax.optimization_barrier(jnp.mean(values, axis=-1, keepdims=True))
    spread = values - center
    variance = lax.optimization_barrier(jnp.mean(spread * spread, axis=-1, keepdims=True))
    return spread * lax.rsqrt(variance + norm_eps) * scales + offsets

def wukong_layer(inputs, up_copy, down_copy, scale_row, offset_row, mixer_row):
    rows_in = FEATS * FM_RANK
    middle = rows_in + MLP_HID
    outer = middle + OUT_TOK * D
    projector = low(mixer_row[:rows_in].reshape(FEATS, FM_RANK))
    compress = low(mixer_row[rows_in:].reshape(LCB_TOK, FEATS))
    inner = low_back(low(jnp.einsum('bnd,nk->bdk', inputs, projector, precision=highest)))
    crossed = low_back(jnp.einsum('bnd,bdk->bnk', inputs, inner, precision=highest))
    crossed = crossed.reshape(inputs.shape[0], rows_in)
    normed = low(layer_norm(crossed, scale_row[:rows_in], offset_row[:rows_in]))
    hidden_pre = low_back(jnp.dot(normed, up_copy, precision=highest) + offset_row[rows_in:middle])
    hidden = low(jax.nn.silu(hidden_pre))
    branch = low_back(jnp.dot(hidden, down_copy, precision=highest) + offset_row[middle:outer])
    branch = branch.reshape(inputs.shape[0], OUT_TOK, D)
    linear = low_back(jnp.einsum('mn,bnd->bmd', compress, inputs, precision=highest))
    summed = inputs + jnp.concatenate([branch, linear], axis=1)
    return layer_norm(summed, scale_row[rows_in:], offset_row[outer:])

def model_loss(weights, nudge, id_rows, mask_rows, label_rows, total):
    table, null_tokens, w_up, w_down, w_top, gains, biases, mixers, top_bias, head = weights
    looked = low_back(low(jnp.take(table, id_rows, axis=0)) + nudge)
    filled = jnp.where(mask_rows[..., None] > 0, looked, null_tokens[None, :, :])
    state = low_back(low(filled))
    for depth in range(2):
        state = wukong_layer(state, low(w_up[depth]), low(w_down[depth]), gains[depth], biases[depth], mixers[depth])
        state = low_back(low(state))
    flat = state.reshape(state.shape[0], FEATS * D)
    top_pre = low_back(jnp.dot(flat, low(w_top), precision=highest) + top_bias)
    top_act = jax.nn.silu(top_pre)
    logits = lax.optimization_barrier(jnp.sum(top_act * head[:TOP_HID], axis=1)) + head[TOP_HID]
    targets = label_rows.astype(jnp.float32)
    losses = jax.nn.softplus(logits) - targets * logits
    return (jnp.sum(losses) / total, losses)

def adam_step(values, grads, first, second, rate, decay):
    first_new = beta_one * first + (1.0 - beta_one) * grads
    second_new = beta_two * second + (1.0 - beta_two) * grads * grads
    first_hat = first_new / (1.0 - beta_one ** STEP)
    second_hat = second_new / (1.0 - beta_two ** STEP)
    values_new = values - rate * (first_hat / (jnp.sqrt(second_hat) + adam_eps) + decay * values)
    return (values_new, first_new, second_new)

def reference(ids, masks, labels, table, table_first, table_second, null_tokens, null_first, null_second, w_up, up_first, up_second, w_down, down_first, down_second, w_top, top_first, top_second, gains, gains_first, gains_second, biases, biases_first, biases_second, mixers, mixers_first, mixers_second, top_bias, top_bias_first, top_bias_second, head, head_first, head_second):
    total = MICRO * EXAMPLES
    params = (table, null_tokens, w_up, w_down, w_top, gains, biases, mixers, top_bias, head)
    sums = tuple((jnp.zeros_like(weight) for weight in params))
    loss_rows = []
    input_rows = []
    for micro_index in range(MICRO):

        def objective(weights, nudge):
            return model_loss(weights, nudge, ids[micro_index], masks[micro_index], labels[micro_index], total)
        nudge = jnp.zeros((EXAMPLES, FEATS, D), jnp.float32)
        _, back, losses = jax.vjp(objective, params, nudge, has_aux=True)
        weight_grads, nudge_grad = back(jnp.ones((), jnp.float32))
        sums = tuple((total_sum + fresh for total_sum, fresh in zip(sums, weight_grads)))
        loss_rows.append(losses)
        input_rows.append(nudge_grad.astype(jnp.bfloat16))
    firsts = (table_first, null_first, up_first, down_first, top_first, gains_first, biases_first, mixers_first, top_bias_first, head_first)
    seconds = (table_second, null_second, up_second, down_second, top_second, gains_second, biases_second, mixers_second, top_bias_second, head_second)
    settings = ((1.0, 0.0), (1.0, 0.0), (0.05, 0.01), (0.05, 0.01), (0.05, 0.01), (1.0, 0.0), (0.1, 0.0), (0.2, 0.01), (0.1, 0.0), (0.1, 0.0))
    results = []
    for group in range(10):
        results.extend(adam_step(params[group], sums[group], firsts[group], seconds[group], settings[group][0], settings[group][1]))
    return (jnp.stack(loss_rows), jnp.stack(input_rows), results[0], results[1], results[2], results[3], results[4], results[5], results[6], results[7], results[8], results[9], results[10], results[11], results[12], results[13], results[14], results[15], results[16], results[17], results[18], results[19], results[20], results[21], results[22], results[23], results[24], results[25], results[26], results[27], results[28], results[29])
```

```python
import functools

import jax
import jax.numpy as jnp
from jax import lax
from jax.experimental import pallas as pl
from jax.experimental.pallas import tpu as pltpu
from jax.sharding import PartitionSpec as P

D = 160
FEATS = 32
OUT_TOK = 16
LCB_TOK = 16
FM_RANK = 24
MLP_HID = 1536
TOP_HID = 2048
STEP = 10


beta_one = 0.9
beta_two = 0.999
adam_eps = 1e-08
norm_eps = 1e-05

MESH = pl.DeviceIdType.MESH
f32 = jnp.float32
bf16 = jnp.bfloat16


def layer_norm(values, scales, offsets):
    center = jnp.mean(values, axis=-1, keepdims=True)
    spread = values - center
    variance = jnp.mean(spread * spread, axis=-1, keepdims=True)
    return spread * lax.rsqrt(variance + norm_eps) * scales + offsets


def adam_step(values, grads, first, second, rate, decay):
    first_new = beta_one * first + (1.0 - beta_one) * grads
    second_new = beta_two * second + (1.0 - beta_two) * grads * grads
    first_hat = first_new / (1.0 - beta_one**STEP)
    second_hat = second_new / (1.0 - beta_two**STEP)
    values_new = values - rate * (first_hat / (jnp.sqrt(second_hat) + adam_eps) + decay * values)
    return (values_new, first_new, second_new)


def split_rows(scale_row, offset_row, mixer_row):
    rows_in = FEATS * FM_RANK
    middle = rows_in + MLP_HID
    outer = middle + OUT_TOK * D
    projector = mixer_row[:rows_in].reshape(FEATS, FM_RANK).astype(jnp.bfloat16)
    compress = mixer_row[rows_in:].reshape(LCB_TOK, FEATS).astype(jnp.bfloat16)
    return (
        scale_row[:rows_in],
        scale_row[rows_in:],
        offset_row[:rows_in],
        offset_row[rows_in:middle],
        offset_row[middle:outer],
        offset_row[outer:],
        projector,
        compress,
    )


def nn(a, b):
    return jnp.dot(a, b, preferred_element_type=f32)


def nt(a, b):
    return lax.dot_general(a, b, (((1,), (1,)), ((), ())), preferred_element_type=f32)


def row_sums(value):
    return jnp.sum(value.reshape(value.shape[0] // 8, 8, value.shape[1]), axis=0)


def all_sum(value):
    return jnp.sum(row_sums(value), axis=0, keepdims=True)


def same_example():
    side = FEATS * 8
    rows = lax.broadcasted_iota(jnp.int32, (side, side), 0)
    columns = lax.broadcasted_iota(jnp.int32, (side, side), 1)
    return (rows & 7) == (columns & 7)


def take_group(ref, start, half):
    pair = ref[:, pl.ds(pl.multiple_of(start, 16), 16), :].astype(f32)
    group = pair[:, 8 * half : 8 * half + 8, :]
    return group.reshape(group.shape[0] * 8, group.shape[2])


def silu_parts(value):
    sigmoid = 1.0 / (1.0 + jnp.exp(-value))
    return value * sigmoid, sigmoid * (1.0 + value * (1.0 - sigmoid))


def layer_copies(depth, up_hbm, down_hbm, up, down, up_sem, down_sem):
    copies = []
    for source, target, sem in ((up_hbm, up, up_sem), (down_hbm, down, down_sem)):
        rows = target.shape[1]
        if len(source.shape) == 3:
            source = source.at[:, pl.ds(depth * rows, rows), :]
        else:
            source = source.at[depth]
        copies.append([pltpu.make_async_copy(source, target, sem)])
    return copies


def all_rows(value):
    return value.reshape(value.shape[0] * value.shape[1], value.shape[2])


def forward_body(
    depth, x_ref, up_hbm, down_hbm, scale_one, offset_one, bias_one, bias_two, scale_two, offset_two, projector, compress,
    next_ref, summed_ref, crossed_ref, normed_back, pre_ref, hidden_back,
    up, down, mixed, linear, branch, normed_ref, hidden_ref, up_sem, down_sem,
):
    batch = x_ref.shape[1]
    up_copies, down_copies = layer_copies(depth, up_hbm, down_hbm, up, down, up_sem, down_sem)
    for copy in up_copies + down_copies:
        copy.start()
    mask = same_example()

    @pl.loop(0, batch // 16)
    def _(g):
        start = pl.multiple_of(g * 16, 16)
        for half in range(2):
            rows = take_group(x_ref, start, half).astype(bf16)
            gram = jnp.where(mask, nt(rows, rows), 0.0).astype(bf16)
            where = pl.ds(pl.multiple_of(start + 8 * half, 8), 8)
            mixed[:, where, :] = nn(gram, projector[...]).reshape(FEATS, 8, FM_RANK)
            linear[:, where, :] = nn(compress[...], rows).reshape(LCB_TOK, 8, D)

    for n in range(FEATS):
        crossed_ref[:, n * FM_RANK : (n + 1) * FM_RANK] = mixed[n]
    crossed = crossed_ref[...]
    normed = layer_norm(crossed, scale_one[...], offset_one[...])
    normed_ref[...] = normed.astype(bf16)
    normed_back[...] = normed.T.astype(bf16)
    for copy in up_copies:
        copy.wait()
    for j in range(0, MLP_HID, 256):
        columns = slice(j, j + 256)
        pre = nn(normed_ref[...], all_rows(up[:, :, columns])) + bias_one[:, columns]
        pre_ref[:, columns] = pre
        hidden = silu_parts(pre)[0]
        hidden_ref[:, columns] = hidden.astype(bf16)
        hidden_back[columns, :] = hidden.T.astype(bf16)
    for copy in down_copies:
        copy.wait()
    for j in range(0, OUT_TOK * D, 256):
        columns = slice(j, j + 256)
        branch[:, columns] = nn(hidden_ref[...], all_rows(down[:, :, columns])) + bias_two[:, columns]
    for n in range(OUT_TOK):
        summed_ref[n] = x_ref[n].astype(f32) + branch[:, n * D : (n + 1) * D]

    @pl.loop(OUT_TOK, FEATS)
    def _(n):
        summed_ref[n] = x_ref[n].astype(f32) + linear[n - OUT_TOK]

    @pl.loop(0, FEATS)
    def _(n):
        next_ref[n] = layer_norm(summed_ref[n], scale_two[...], offset_two[...]).astype(bf16)


def backward_body(
    depth, upstream, x_ref, summed, crossed_ref, pre_ref, up_hbm, down_hbm, scale_one, scale_two, projector, compress,
    compress_back,
    grad_x, branch_ref, grad_pre, scales_out, offsets_out, mixers_out,
    up, down, sums, branch, crossed_grad, mixed, scale_two_sum, offset_two_sum, projector_sum, compress_sum,
    up_sem, down_sem,
):
    batch = x_ref.shape[1]
    up_copies, down_copies = layer_copies(depth, up_hbm, down_hbm, up, down, up_sem, down_sem)
    for copy in down_copies + up_copies:
        copy.start()
    mask = same_example()
    rows_in = FEATS * FM_RANK
    middle = rows_in + MLP_HID
    scale_two_sum[...] = jnp.zeros_like(scale_two_sum)
    offset_two_sum[...] = jnp.zeros_like(offset_two_sum)
    projector_sum[...] = jnp.zeros_like(projector_sum)
    compress_sum[...] = jnp.zeros_like(compress_sum)

    @pl.loop(0, FEATS)
    def _(n):
        value = summed[n]
        above = upstream[n].astype(f32)
        spread = value - jnp.mean(value, axis=-1, keepdims=True)
        inverse = lax.rsqrt(jnp.mean(spread * spread, axis=-1, keepdims=True) + norm_eps)
        unit = spread * inverse
        scaled = above * scale_two[...]
        scale_two_sum[...] += row_sums(above * unit)
        offset_two_sum[...] += row_sums(above)
        sums[n] = inverse * (
            scaled
            - jnp.mean(scaled, axis=-1, keepdims=True)
            - unit * jnp.mean(scaled * unit, axis=-1, keepdims=True)
        )

    for n in range(OUT_TOK):
        branch[:, n * D : (n + 1) * D] = sums[n]
    for j in range(0, OUT_TOK * D, 256):
        columns = slice(j, j + 256)
        rounded = branch[:, columns].astype(bf16)
        branch_ref[:, columns] = rounded
        offsets_out[:, middle + j : middle + j + 256] = all_sum(rounded.astype(f32))
    for copy in down_copies:
        copy.wait()
    part_rows = down.shape[1]
    step = 2 * part_rows if down.shape[0] > 1 else 256
    for j in range(0, MLP_HID, step):
        columns = slice(j, j + step)
        if down.shape[0] > 1:
            weights = all_rows(down[j // part_rows : (j + step) // part_rows])
        else:
            weights = down[0, columns, :]
        below = nt(branch_ref[...], weights) * silu_parts(pre_ref[:, columns])[1]
        rounded = below.astype(bf16)
        grad_pre[:, columns] = rounded
        offsets_out[:, rows_in + j : rows_in + j + step] = all_sum(rounded.astype(f32))
    for copy in up_copies:
        copy.wait()
    crossed = crossed_ref[...]
    above = nt(grad_pre[...], all_rows(up[...]))
    spread = crossed - jnp.mean(crossed, axis=-1, keepdims=True)
    inverse = lax.rsqrt(jnp.mean(spread * spread, axis=-1, keepdims=True) + norm_eps)
    unit = spread * inverse
    scaled = above * scale_one[...]
    scales_out[:, :rows_in] = all_sum(above * unit)
    offsets_out[:, :rows_in] = all_sum(above)
    crossed_grad[...] = inverse * (
        scaled
        - jnp.mean(scaled, axis=-1, keepdims=True)
        - unit * jnp.mean(scaled * unit, axis=-1, keepdims=True)
    )
    for n in range(FEATS):
        mixed[n] = crossed_grad[:, n * FM_RANK : (n + 1) * FM_RANK]

    @pl.loop(0, batch // 16)
    def _(g):
        start = pl.multiple_of(g * 16, 16)
        parts = []
        for half in range(2):
            rows = take_group(x_ref, start, half).astype(bf16)
            where = pl.ds(pl.multiple_of(start + 8 * half, 8), 8)
            above = mixed[:, where, :].reshape(FEATS * 8, FM_RANK).astype(bf16)
            direct = sums[:, where, :].reshape(FEATS * 8, D)
            tail = direct[OUT_TOK * 8 :].astype(bf16)
            gram = jnp.where(mask, nt(rows, rows), 0.0).astype(bf16)
            projector_sum[...] += nn(gram, above)
            compress_sum[...] += nt(tail, rows)
            weights = projector[...]
            both = jnp.where(mask, nt(above, weights) + nt(weights, above), 0.0).astype(bf16)
            total = direct + nn(both, rows) + nn(compress_back[...], tail)
            parts.append(total.reshape(FEATS, 8, D))
        grad_x[:, pl.ds(start, 16), :] = jnp.concatenate(parts, axis=1).astype(bf16)

    scales_out[:, rows_in:] = jnp.sum(scale_two_sum[...], axis=0, keepdims=True)
    offsets_out[:, middle + OUT_TOK * D :] = jnp.sum(offset_two_sum[...], axis=0, keepdims=True)
    by_token = jnp.sum(projector_sum[...].reshape(FEATS, 8, FM_RANK), axis=1)
    for n in range(FEATS):
        mixers_out[:, n * FM_RANK : (n + 1) * FM_RANK] = by_token[n : n + 1]
    own_example = jnp.where(mask[: LCB_TOK * 8], compress_sum[...], 0.0)
    by_row = jnp.sum(own_example.reshape(LCB_TOK, 8, FEATS * 8), axis=1)
    side = FEATS * 8
    fold = lax.broadcasted_iota(jnp.int32, (side, FEATS), 0) // 8
    fold = (fold == lax.broadcasted_iota(jnp.int32, (side, FEATS), 1)).astype(f32)
    by_pair = jnp.dot(by_row, fold, preferred_element_type=f32, precision=lax.Precision.HIGHEST)
    for n in range(LCB_TOK):
        mixers_out[:, rows_in + n * FEATS : rows_in + (n + 1) * FEATS] = by_pair[n : n + 1]


def top_body(
    x_ref, weight_hbm, bias, head, targets, total,
    flat_back, logits_ref, grad_pre, grad_x, bias_out, head_out,
    weight, flat, flat_ref, pre, piece, sem,
):
    tile = 256
    copies = [
        pltpu.make_async_copy(
            weight_hbm.at[:, pl.ds(j * tile, tile)], weight.at[:, pl.ds(j * tile, tile)], sem.at[j]
        )
        for j in range(TOP_HID // tile)
    ]
    for copy in copies:
        copy.start()
    for n in range(FEATS):
        token = x_ref[n].astype(f32)
        flat[:, n * D : (n + 1) * D] = token
        flat_back[n * D : (n + 1) * D, :] = token.T.astype(bf16)
    for j in range(0, FEATS * D, 256):
        flat_ref[:, j : j + 256] = flat[:, j : j + 256].astype(bf16)
    logits = jnp.zeros((x_ref.shape[1], 1), f32)
    for j, copy in enumerate(copies):
        columns = slice(j * tile, (j + 1) * tile)
        copy.wait()
        value = nn(flat_ref[...], weight[:, columns]) + bias[:, columns]
        pre[:, columns] = value
        logits += jnp.sum(silu_parts(value)[0] * head[:, columns], axis=1, keepdims=True)
    logits = logits + head[:, TOP_HID : TOP_HID + 1]
    logits_ref[...] = logits
    grad_logits = (1.0 / (1.0 + jnp.exp(-logits)) - targets[...]) / total
    for j in range(0, TOP_HID, tile):
        columns = slice(j, j + tile)
        act, slope = silu_parts(pre[:, columns])
        rounded = (grad_logits * head[:, columns] * slope).astype(bf16)
        grad_pre[:, columns] = rounded
        bias_out[:, columns] = all_sum(rounded.astype(f32))
        head_out[:, columns] = all_sum(act * grad_logits)
    for j in range(0, FEATS, 4):
        piece[...] = nt(grad_pre[...], weight[j * D : (j + 4) * D, :])
        for k in range(4):
            grad_x[j + k] = piece[:, k * D : (k + 1) * D].astype(bf16)


def whole(count):
    return [pl.BlockSpec(memory_space=pltpu.VMEM)] * count


def in_place(count):
    return [pl.BlockSpec(memory_space=pl.ANY)] * count


def kernel_params():
    return pltpu.CompilerParams(vmem_limit_bytes=60 * 1024 * 1024)


def layer_values(scale_row, offset_row, mixer_row):
    scale_one, scale_two, offset_one, bias_one, bias_two, offset_two, projector, compress = split_rows(
        scale_row, offset_row, mixer_row
    )
    wide = jnp.repeat(projector, 8, axis=0)
    mixing = jnp.kron(compress.astype(f32), jnp.eye(8, dtype=f32)).astype(bf16)
    rows = [part[None, :] for part in (scale_one, offset_one, bias_one, bias_two, scale_two, offset_two)]
    return rows, wide, mixing


def layer_forward(depth, inputs, up_copy, down_copy, values):
    rows, wide, mixing = values
    batch = inputs.shape[1]
    parts = up_copy.shape[0] if len(up_copy.shape) == 3 else 1
    shape = jax.ShapeDtypeStruct
    return pl.pallas_call(
        functools.partial(forward_body, depth),
        out_shape=[
            shape((FEATS, batch, D), bf16),
            shape((FEATS, batch, D), f32),
            shape((batch, FEATS * FM_RANK), f32),
            shape((FEATS * FM_RANK, batch), bf16),
            shape((batch, MLP_HID), f32),
            shape((MLP_HID, batch), bf16),
        ],
        in_specs=whole(1) + in_place(2) + whole(8),
        out_specs=whole(6),
        scratch_shapes=[
            pltpu.VMEM((parts, FEATS * FM_RANK // parts, MLP_HID), bf16),
            pltpu.VMEM((parts, MLP_HID // parts, OUT_TOK * D), bf16),
            pltpu.VMEM((FEATS, batch, FM_RANK), f32),
            pltpu.VMEM((LCB_TOK, batch, D), f32),
            pltpu.VMEM((batch, OUT_TOK * D), f32),
            pltpu.VMEM((batch, FEATS * FM_RANK), bf16),
            pltpu.VMEM((batch, MLP_HID), bf16),
            pltpu.SemaphoreType.DMA(()),
            pltpu.SemaphoreType.DMA(()),
        ],
        compiler_params=kernel_params(),
        name="layer_forward",
    )(inputs, up_copy, down_copy, *rows, wide, mixing)


def layer_backward(depth, upstream, inputs, stored, up_copy, down_copy, values):
    rows, wide, mixing = values
    summed, crossed, normed, pre, hidden = stored
    batch = inputs.shape[1]
    parts = up_copy.shape[0] if len(up_copy.shape) == 3 else 1
    shape = jax.ShapeDtypeStruct
    outs = pl.pallas_call(
        functools.partial(backward_body, depth),
        out_shape=[
            shape((FEATS, batch, D), bf16),
            shape((batch, OUT_TOK * D), bf16),
            shape((batch, MLP_HID), bf16),
            shape((1, FEATS * FM_RANK + D), f32),
            shape((1, FEATS * FM_RANK + MLP_HID + OUT_TOK * D + D), f32),
            shape((1, FEATS * FM_RANK + LCB_TOK * FEATS), f32),
        ],
        in_specs=whole(5) + in_place(2) + whole(5),
        out_specs=whole(6),
        scratch_shapes=[
            pltpu.VMEM((parts, FEATS * FM_RANK // parts, MLP_HID), bf16),
            pltpu.VMEM((parts, MLP_HID // parts, OUT_TOK * D), bf16),
            pltpu.VMEM((FEATS, batch, D), f32),
            pltpu.VMEM((batch, OUT_TOK * D), f32),
            pltpu.VMEM((batch, FEATS * FM_RANK), f32),
            pltpu.VMEM((FEATS, batch, FM_RANK), f32),
            pltpu.VMEM((8, D), f32),
            pltpu.VMEM((8, D), f32),
            pltpu.VMEM((FEATS * 8, FM_RANK), f32),
            pltpu.VMEM((LCB_TOK * 8, FEATS * 8), f32),
            pltpu.SemaphoreType.DMA(()),
            pltpu.SemaphoreType.DMA(()),
        ],
        compiler_params=kernel_params(),
        name="layer_backward",
    )(upstream, inputs, summed, crossed, pre, up_copy, down_copy, rows[0], rows[4], wide, mixing, mixing.T)
    grad_x, grad_branch, grad_pre, scales, offsets, mixers = outs
    grad_up, grad_down = (normed, grad_pre), (hidden, grad_branch)
    return (
        grad_x,
        grad_up,
        grad_down,
        scales[0],
        offsets[0],
        mixers[0],
    )


def top_pass(inputs, top_copy, top_bias, head, targets, total):
    batch = inputs.shape[1]
    shape = jax.ShapeDtypeStruct
    flat, logits, grad_pre, grad_x, bias_sums, head_sums = pl.pallas_call(
        lambda *refs: top_body(*refs[:5], float(total), *refs[5:]),
        out_shape=[
            shape((FEATS * D, batch), bf16),
            shape((batch, 1), f32),
            shape((batch, TOP_HID), bf16),
            shape((FEATS, batch, D), bf16),
            shape((1, TOP_HID), f32),
            shape((1, TOP_HID), f32),
        ],
        in_specs=whole(1) + in_place(1) + whole(3),
        out_specs=whole(6),
        scratch_shapes=[
            pltpu.VMEM((FEATS * D, TOP_HID), bf16),
            pltpu.VMEM((batch, FEATS * D), f32),
            pltpu.VMEM((batch, FEATS * D), bf16),
            pltpu.VMEM((batch, TOP_HID), f32),
            pltpu.VMEM((batch, 4 * D), f32),
            pltpu.SemaphoreType.DMA((TOP_HID // 256,)),
        ],
        compiler_params=kernel_params(),
        name="top_pass",
    )(inputs, top_copy, top_bias[None, :], head[None, :], targets[:, None])
    logits = logits[:, 0]
    losses = jax.nn.softplus(logits) - targets * logits
    grad_logits = (jax.nn.sigmoid(logits) - targets) / total
    grad_head = jnp.concatenate([head_sums[0], jnp.sum(grad_logits)[None]])
    return losses, grad_x, (flat, grad_pre), bias_sums[0], grad_head


def gather_rows(matrix, section_index, sections, axis):
    rows = matrix.shape[axis] // sections
    piece = lax.dynamic_slice_in_dim(matrix, section_index * rows, rows, axis).astype(bf16)
    return lax.all_gather(piece, ("dp", "section"), axis=axis, tiled=True)


def chunk_rows(rows, weight, limit):
    best = rows
    for size in range(16, rows + 1, 16):
        if rows % size == 0 and (rows // size) % 2 == 0 and size * weight <= limit:
            best = size
    return best


def reduce_plan(shapes, members, plane_shapes):
    plan = []
    for index, (rows, cols) in enumerate(shapes):
        size = chunk_rows(rows, cols * members, 700000)
        plan += [(index, start, size, cols // 4, members // 2) for start in range(0, rows, size)]
    for index, (rows, cols) in enumerate(plane_shapes):
        size = chunk_rows(rows // 4, cols, 50000)
        plan += [
            (len(shapes) + index, start, size, cols, 1) for start in range(0, rows // 4, size)
        ]
    return plan


def ring_slots(plan):
    slots, ring, seen = [], [], {}
    for chunk in plan:
        *_, deep = chunk
        mine = seen.setdefault(chunk[2:], [])
        if deep == 1 or len(mine) < 6:
            ring.append(chunk)
            slots.append(len(ring) - 1)
        else:
            slots.append(mine[len(mine) % 6])
        mine.append(slots[-1])
    return slots, ring


def reduce_body(plan, slots, counts, members, *refs):
    matrices, planes, swaps, smalls = counts
    count = matrices + planes + swaps + smalls
    lefts, refs = refs[:matrices], refs[matrices:]
    inputs, outs, scratch = refs[:count], refs[count : 2 * count], refs[2 * count :]
    total = len(plan)
    stacks = members // 2
    ring = max(slots) + 1
    mixed, half = ([scratch[k * ring + slot] for slot in slots] for k in range(2))
    scratch = scratch[2 * ring :]
    first_in, second_in, quarter, done = (scratch[k * total : (k + 1) * total] for k in range(4))
    scratch = scratch[4 * total :]
    left, right, left_in, right_in = (scratch[k * matrices : (k + 1) * matrices] for k in range(4))
    stack_in = scratch[4 * matrices : 4 * matrices + sum(index < matrices for index, *_ in plan)]
    own_sem, side_sem, side_send, side_recv, pair_send, pair_recv, stack_send, stack_recv, out_send, out_recv, keep_sem, swap_send, swap_recv, swap_keep = (
        scratch[4 * matrices + len(stack_in) : 4 * matrices + len(stack_in) + 14]
    )
    small_now, small_in = scratch[-2 - 2 * smalls : -2 - smalls], scratch[-2 - smalls : -2]
    small_send, small_recv = scratch[-2:]
    section, member = lax.axis_index("section"), lax.axis_index("dp")
    stack, core = member // 2, member % 2
    x, y = section % 2, section // 2
    sibling = (section, member + 1 - 2 * core)
    beside_x = (section + 1 - 2 * x, member)
    beside_y = (section + 2 - 4 * y, member)
    others = [beside_x, beside_y, (3 - section, member)]
    peers = [(section, lax.rem(stack + k, stacks) * 2 + core) for k in range(1, stacks)]
    line = [(section, lax.rem(member + k, members)) for k in range(1, members)]

    barrier = pltpu.get_barrier_semaphore()
    partners = others + (line if swaps else [sibling] + peers)
    for device in partners:
        pl.semaphore_signal(barrier, inc=1, device_id=device, device_id_type=MESH)
    pl.semaphore_wait(barrier, len(partners))

    def remote(source, target, send, recv, device):
        return pltpu.make_async_remote_copy(
            src_ref=source, dst_ref=target, send_sem=send, recv_sem=recv, device_id=device, device_id_type=MESH
        )

    def own_copy(i):
        index, start, size, *_ = plan[i]
        return pltpu.make_async_copy(
            inputs[index].at[:, pl.ds(start, size), :], mixed[i], own_sem.at[i]
        )

    def side_copies(m):
        return [
            pltpu.make_async_copy(lefts[m].at[:, core], left[m], side_sem.at[m, 0]),
            pltpu.make_async_copy(inputs[m], right[m], side_sem.at[m, 1]),
            remote(lefts[m].at[:, 1 - core], left_in[m], side_send.at[m, 0], side_recv.at[m, 0], sibling),
            remote(inputs[m], right_in[m], side_send.at[m, 1], side_recv.at[m, 1], sibling),
        ]

    def first_copy(i):
        deep = plan[i][4]
        if i % 2 == 0:
            blocks = [(2 * t + 1 - x, t) for t in range(2)]
        else:
            blocks = [(2 * (1 - y) + t, t) for t in range(2)]
        return [
            remote(
                mixed[i].at[pl.ds(block * deep, deep)],
                first_in[i].at[t],
                pair_send.at[i, t],
                pair_recv.at[i, t],
                beside_x if i % 2 == 0 else beside_y,
            )
            for block, t in blocks
        ]

    def second_copy(i):
        source, device = (
            (half[i].at[1 - y], beside_y) if i % 2 == 0 else (half[i].at[1 - x], beside_x)
        )
        return remote(source, second_in[i], pair_send.at[i, 2], pair_recv.at[i, 2], device)

    def stack_copy(i, k):
        return remote(
            quarter[i].at[lax.rem(stack + k + 1, stacks)],
            stack_in[i].at[k],
            stack_send.at[i, k],
            stack_recv.at[i, k],
            peers[k],
        )

    def place(i, which):
        index, start, size, width, _ = plan[i]
        if index >= matrices:
            rows = outs[index].shape[0] // 4
            return outs[index].at[pl.ds(pl.multiple_of(which * rows + start, 16), size), :]
        columns = pl.ds(pl.multiple_of(which * width, 128), width)
        return outs[index].at[pl.ds(start, size), columns]

    def out_copy(i, k, arrived=False):
        first, second = (beside_x, beside_y) if i % 2 == 0 else (beside_y, beside_x)
        sent = place(i, (section, section, first[0])[k])
        came = place(i, (first[0], second[0], 3 - section)[k])
        source = sent if k == 2 else done[i]
        return remote(
            source, came if arrived else sent, out_send.at[i, k], out_recv.at[i, k], second if k else first
        )

    def keep_copy(i):
        return pltpu.make_async_copy(done[i], place(i, section), keep_sem.at[i])

    def swap_copy(j, k):
        index = matrices + planes + j
        return remote(
            inputs[index].at[lax.rem(member + k + 1, members)],
            outs[index].at[member],
            swap_send.at[j, k],
            swap_recv.at[j, k],
            line[k],
        )

    def swap_arrival(j, k):
        index = matrices + planes + j
        return remote(
            inputs[index].at[member],
            outs[index].at[lax.rem(member + members - k - 1, members)],
            swap_send.at[j, k],
            swap_recv.at[j, k],
            line[k],
        )

    def swap_own(j):
        index = matrices + planes + j
        return pltpu.make_async_copy(
            inputs[index].at[member], outs[index].at[member], swap_keep.at[j]
        )

    across_stacks = [
        (section, (stack + step - 2 * step * (stack // step % 2)) * 2 + core)
        for step in (1, 2, 4)
        if step < stacks
    ]
    pairs = [sibling, beside_x, beside_y] + across_stacks

    def small_copy(j, t):
        return remote(small_now[j], small_in[j].at[t], small_send.at[j, t], small_recv.at[j, t], pairs[t])

    def small_first(j):
        return pltpu.make_async_copy(inputs[count - smalls + j], small_now[j], small_send.at[j, 0])

    def small_last(j):
        return pltpu.make_async_copy(small_now[j], outs[count - smalls + j], small_send.at[j, 0])

    def stage_small(t):
        for j in range(smalls):
            if t == 0:
                small_first(j).wait()
            else:
                small_copy(j, t - 1).wait()
                small_now[j][...] += small_in[j][t - 1]
        for j in range(smalls):
            if t < len(pairs):
                small_copy(j, t).start()
            else:
                small_last(j).start()

    def stage_product(i):
        index, start, size, width, deep = plan[i]
        if index >= matrices:
            own_copy(i).wait()
        else:
            if start == 0:
                for copy in side_copies(index):
                    copy.wait()
            twice = i + 1 < total and plan[i + 1][:3] == (index, start + size, size)
            if start // size % 2 == 0:
                reach = 2 * size if twice else size
                rows = slice(start, start + reach)
                mine, other = all_rows(left[index][:, rows, :]), all_rows(left_in[index][:, rows, :])
                for s in range(4):
                    columns = slice(s * width, (s + 1) * width)
                    value = nn(mine, right[index][:, columns]) + nn(other, right_in[index][:, columns])
                    value = value.astype(bf16).reshape(deep, reach, width)
                    mixed[i][s * deep : (s + 1) * deep] = value[:, :size]
                    if twice:
                        mixed[i + 1][s * deep : (s + 1) * deep] = value[:, size:]

        for copy in first_copy(i):
            copy.start()

    def stage_first(i):
        deep = plan[i][4]
        for copy in first_copy(i):
            copy.wait()

        @pl.loop(0, deep)
        def _(z):
            for t in range(2):
                block = 2 * t + x if i % 2 == 0 else 2 * y + t
                mine = mixed[i][block * deep + z]
                half[i][t, z] = (mine.astype(f32) + first_in[i][t, z].astype(f32)).astype(bf16)

        second_copy(i).start()

    def stage_second(i):
        deep = plan[i][4]
        second_copy(i).wait()

        @pl.loop(0, deep)
        def _(z):
            mine = half[i][y, z] if i % 2 == 0 else half[i][x, z]
            quarter[i][z] = (mine.astype(f32) + second_in[i][z].astype(f32)).astype(bf16)

        for k in range(deep - 1):
            stack_copy(i, k).start()

    def stage_stack(i):
        deep = plan[i][4]
        for k in range(deep - 1):
            stack_copy(i, k).wait()
        value = quarter[i][stack if deep > 1 else 0].astype(f32)
        for k in range(deep - 1):
            value = value + stack_in[i][k].astype(f32)
        done[i][...] = value.astype(bf16)
        keep_copy(i).start()
        out_copy(i, 0).start()

    def stage_out(i):
        out_copy(i, 0, True).wait_recv()
        for k in (1, 2):
            out_copy(i, k).start()

    lag = 3
    for j in range(smalls):
        small_first(j).start()
    for m in range(matrices):
        for copy in side_copies(m):
            copy.start()
    for i in range(total):
        if plan[i][0] >= matrices:
            own_copy(i).start()
    for j in range(swaps):
        swap_own(j).start()
    patience = 6 if swaps else lag
    lags = (0, lag, 2 * lag, 2 * lag + patience, 3 * lag + patience)
    stages = tuple(zip(lags, (stage_product, stage_first, stage_second, stage_stack, stage_out)))
    for step in range(total + lags[-1]):
        if step % 4 == 0 and step // 4 < members - 1:
            for j in range(swaps):
                swap_copy(j, step // 4).start()
        for behind, stage in stages:
            if 0 <= step - behind < total:
                stage(step - behind)
        if smalls and step % 3 == 0 and step // 3 <= len(pairs):
            stage_small(step // 3)
    for i in range(total):
        keep_copy(i).wait()
        for k in range(3):
            out_copy(i, k).wait_send()
            if k:
                out_copy(i, k, True).wait_recv()
    for j in range(smalls):
        small_last(j).wait()
    for j in range(swaps):
        swap_own(j).wait()
        for k in range(members - 1):
            swap_copy(j, k).wait_send()
            swap_arrival(j, k).wait_recv()


def reduce_kernel(pairs, planes, swaps, smalls, members, collective_id):
    stacks = members // 2
    count = len(pairs)
    shapes = [(left.shape[0] // members, right.shape[1]) for left, right in pairs]
    plan = reduce_plan(shapes, members, [part.shape for part in planes])
    total, matrix_chunks = len(plan), sum(index < count for index, *_ in plan)
    lefts = [left.reshape(stacks, 2, -1, left.shape[1]) for left, _ in pairs]
    inputs = [right for _, right in pairs]
    inputs += [part.reshape((4, part.shape[0] // 4, part.shape[1])) for part in planes]
    inputs += list(swaps) + list(smalls)
    steps = 3 + (stacks - 1).bit_length()

    slots, ring = ring_slots(plan)

    def buffers(lead, chunks=plan):
        return [pltpu.VMEM(lead(deep) + (size, width), bf16) for _, _, size, width, deep in chunks]

    sides = [pltpu.VMEM((stacks,) + left.shape[2:], bf16) for left in lefts]
    sides += [pltpu.VMEM(right.shape, bf16) for _, right in pairs]
    across = [
        pltpu.VMEM((deep - 1, size, width), bf16) for _, _, size, width, deep in plan[:matrix_chunks]
    ]
    dma = pltpu.SemaphoreType.DMA
    swap_count = max(len(swaps), 1)
    return pl.pallas_call(
        functools.partial(
            reduce_body, plan, slots, (count, len(planes), len(swaps), len(smalls)), members
        ),
        out_shape=[jax.ShapeDtypeStruct(shape, bf16) for shape in shapes]
        + [jax.ShapeDtypeStruct(part.shape, part.dtype) for part in (*planes, *swaps, *smalls)],
        in_specs=in_place(count + len(inputs)),
        out_specs=in_place(len(inputs)),
        scratch_shapes=buffers(lambda deep: (4 * deep,), ring)
        + buffers(lambda deep: (2, deep), ring)
        + buffers(lambda deep: (2, deep))
        + buffers(lambda deep: (deep,)) * 2
        + buffers(lambda deep: ())
        + sides * 2
        + across
        + [
            dma((total,)),
            dma((max(count, 1), 2)),
            dma((max(count, 1), 2)),
            dma((max(count, 1), 2)),
            dma((total, 3)),
            dma((total, 3)),
            dma((total, stacks - 1)),
            dma((total, stacks - 1)),
            dma((total, 3)),
            dma((total, 3)),
            dma((total,)),
            dma((swap_count, members - 1)),
            dma((swap_count, members - 1)),
            dma((swap_count,)),
        ]
        + [pltpu.VMEM(part.shape, f32) for part in smalls]
        + [pltpu.VMEM((steps,) + part.shape, f32) for part in smalls]
        + [dma((max(len(smalls), 1), steps))] * 2,
        compiler_params=pltpu.CompilerParams(
            collective_id=collective_id, has_side_effects=True, vmem_limit_bytes=60 * 1024 * 1024
        ),
        name="reduce_rows",
    )(*lefts, *inputs)


MAIN = 128
TAIL = D - MAIN


def pack_body(members, slots, rows_ref, main_ref, tail_ref, main, tail):
    capacity = main_ref.shape[1]
    part = capacity // 4
    main[...] = jnp.zeros_like(main)
    tail[...] = jnp.zeros_like(tail)

    @pl.loop(0, rows_ref.shape[0] // 16)
    def _(i):
        start = pl.multiple_of(i * 16, 16)
        block = rows_ref[pl.ds(start, 16), :].astype(f32)
        for u in range(16):
            slot = pl.ds(slots[start + u], 1)
            main[slot, :] = block[u : u + 1, :MAIN]
            tail[slot, :] = block[u : u + 1, MAIN:]

    @pl.loop(0, members)
    def _(k):
        start = pl.multiple_of(k * capacity, 16)
        main_ref[k] = main[pl.ds(start, capacity), :].astype(bf16)
        pieces = [tail[pl.ds(start + j * part, part), :] for j in range(4)]
        tail_ref[k] = jnp.concatenate(pieces, axis=1).astype(bf16)


def pack_rows(rows, slots, members, capacity):
    shape = jax.ShapeDtypeStruct
    return pl.pallas_call(
        functools.partial(pack_body, members),
        out_shape=[shape((members, capacity, MAIN), bf16), shape((members, capacity // 4, MAIN), bf16)],
        in_specs=[pl.BlockSpec(memory_space=pltpu.SMEM)] + whole(1),
        out_specs=whole(2),
        scratch_shapes=[
            pltpu.VMEM((members * capacity, MAIN), f32),
            pltpu.VMEM((members * capacity, TAIL), f32),
        ],
        compiler_params=kernel_params(),
        name="pack_rows",
    )(slots, rows)


def add_body(members, asked, counts, main_ref, tail_ref, main_out, tail_out, main, tail, *sums):
    capacity = main_ref.shape[1]
    part = capacity // 4
    for total in sums:
        total[...] = jnp.zeros_like(total)

    @pl.loop(0, members)
    def _(k):
        start = pl.multiple_of(k * capacity, 16)
        main[pl.ds(start, capacity), :] = main_ref[k].astype(f32)
        wide = tail_ref[k].astype(f32)
        for j in range(4):
            tail[pl.ds(start + j * part, part), :] = wide[:, j * TAIL : (j + 1) * TAIL]

    @pl.loop(0, members)
    def _(k):
        @pl.loop(0, (counts[k] + 3) // 4)
        def _(i):
            for u in range(4):
                j = k * capacity + i * 4 + u
                here, there = pl.ds(j, 1), pl.ds(asked[j], 1)
                sums[2 * u][there, :] += main[here, :]
                sums[2 * u + 1][there, :] += tail[here, :]

    rows = main_out.shape[0] // 4
    tiles = []
    for j in range(4):
        where = slice(j * rows, (j + 1) * rows)
        main_out[where, :] = (
            sums[0][where, :] + sums[2][where, :] + sums[4][where, :] + sums[6][where, :]
        ).astype(bf16)
        tiles.append(sums[1][where, :] + sums[3][where, :] + sums[5][where, :] + sums[7][where, :])
    tail_out[...] = jnp.concatenate(tiles, axis=1).astype(bf16)


def add_rows(main, tail, asked, counts, rows):
    members, capacity, _ = main.shape
    shape = jax.ShapeDtypeStruct
    smem = pl.BlockSpec(memory_space=pltpu.SMEM)
    return pl.pallas_call(
        functools.partial(add_body, members),
        out_shape=[shape((rows, MAIN), bf16), shape((rows // 4, MAIN), bf16)],
        in_specs=[smem, smem] + whole(2),
        out_specs=whole(2),
        scratch_shapes=[
            pltpu.VMEM((members * capacity, MAIN), f32),
            pltpu.VMEM((members * capacity, TAIL), f32),
        ]
        + [pltpu.VMEM((rows, MAIN), f32), pltpu.VMEM((rows, TAIL), f32)] * 4,
        compiler_params=kernel_params(),
        name="add_rows",
    )(asked, counts, main, tail)


def gather_body(members, plan, counts, *refs):
    matrices, swaps = counts
    count = matrices + swaps
    inputs, outs = refs[:count], refs[count : 2 * count]
    next_send, pass_send, stack_recv, pair_send, pair_recv, core_send, core_recv, own_send, own_recv, keep, swap_send, swap_recv = (
        refs[2 * count :]
    )
    stacks = members // 2
    section, member = lax.axis_index("section"), lax.axis_index("dp")
    stack, core = member // 2, member % 2
    x, y = section % 2, section // 2
    sibling = (section, member + 1 - 2 * core)
    over_x, over_y = section + 1 - 2 * x, section + 2 - 4 * y
    line = [(section, lax.rem(member + k, members)) for k in range(1, members)]
    partners = [(over_x, member), (over_y, member)] + line
    barrier = pltpu.get_barrier_semaphore()
    for device in partners:
        pl.semaphore_signal(barrier, inc=1, device_id=device, device_id_type=MESH)
    pl.semaphore_wait(barrier, len(partners))

    def remote(source, target, send, recv, device):
        return pltpu.make_async_remote_copy(
            src_ref=source, dst_ref=target, send_sem=send, recv_sem=recv, device_id=device, device_id_type=MESH
        )

    pieces = len(plan)
    if stacks == 4:
        lowest, highest = 1 - (stack + 3) // 4, (stack + 1) // 4
        by_distance = [1 + 2 * lowest, 3 - lowest - highest, 2 - lowest + highest]
    else:
        by_distance = list(range(1, stacks))
    units = [(i, k) for i in range(pieces) for k in by_distance]

    def unit(i, k):
        return i * (stacks - 1) + k - 1

    def block(i, owner_stack, which_core, which_section):
        index, start, size, width = plan[i]
        owner = owner_stack * 2 + which_core
        if which_section is None:
            return outs[index].at[owner, pl.ds(start, size), :]
        columns = pl.ds(pl.multiple_of(which_section * width, 128), width)
        return outs[index].at[owner, pl.ds(start, size), columns]

    def from_stack_of(k):
        return lax.rem(stack + stacks - k, stacks)

    def beyond(up):
        return (section, member + (2 if up else -2))

    def next_copy(i, up):
        index, start, size, width = plan[i]
        columns = pl.ds(pl.multiple_of(section * width, 128), width)
        source = inputs[index].at[pl.ds(start, size), columns]
        there = unit(i, 1 if up else stacks - 1)
        return remote(
            source, block(i, stack, core, section), next_send.at[i, int(up)], stack_recv.at[there], beyond(up)
        )

    def pass_copy(i, k, up):
        here = block(i, from_stack_of(k), core, section)
        there = unit(i, k + 1 if up else k - 1)
        return remote(here, here, pass_send.at[unit(i, k)], stack_recv.at[there], beyond(up))

    def arrival(i, k):
        here = block(i, from_stack_of(k), core, section)
        return remote(here, here, pass_send.at[unit(i, k)], stack_recv.at[unit(i, k)], sibling)

    def goes(k, up):
        if up:
            return (stack >= k) & (stack < stacks - 1)
        return (stack < k) & (stack > 0)

    def pair_copy(u, which, arrived):
        i, k = units[u]
        first, second = (over_x, over_y) if u % 2 == 0 else (over_y, over_x)
        owner = from_stack_of(k)
        here = block(i, owner, core, (section, section, first)[which])
        came = block(i, owner, core, (first, second, 3 - section)[which])
        device = (first if which == 0 else second, member)
        return remote(
            here, came if arrived else here, pair_send.at[u, which], pair_recv.at[u, which], device
        )

    def core_copy(u, arrived):
        i, k = units[u]
        here = block(i, from_stack_of(k), core, None)
        came = block(i, from_stack_of(k), 1 - core, None)
        return remote(here, came if arrived else here, core_send.at[u], core_recv.at[u], sibling)

    def own_copy(m, arrived):
        target = outs[m].at[member + 1 - 2 * core] if arrived else outs[m].at[member]
        return remote(inputs[m], target, own_send.at[m], own_recv.at[m], sibling)

    def swap_copy(j, k, arrived):
        target = lax.rem(member + members - k - 1, members) if arrived else member
        return remote(
            inputs[matrices + j].at[lax.rem(member + k + 1, members)],
            outs[matrices + j].at[target],
            swap_send.at[j, k],
            swap_recv.at[j, k],
            line[k],
        )

    kept = [pltpu.make_async_copy(inputs[m], outs[m].at[member], keep.at[m]) for m in range(matrices)]
    kept += [
        pltpu.make_async_copy(inputs[j].at[member], outs[j].at[member], keep.at[j])
        for j in range(matrices, count)
    ]

    def both_ways(chosen, act):
        for i in chosen:
            for up in (True, False):

                @pl.when((stack < stacks - 1) if up else (stack > 0))
                def _():
                    act(next_copy(i, up))

    ahead = 2
    both_ways(range(min(ahead, pieces)), lambda copy: copy.start())
    for copy in kept:
        copy.start()

    def passing(u, act):
        i, k = units[u]
        for up in (True, False):

            @pl.when(goes(k, up))
            def _():
                act(pass_copy(i, k, up))

    def from_stack(u):
        arrival(*units[u]).wait_recv()
        passing(u, lambda copy: copy.start())
        pair_copy(u, 0, False).start()

    def from_first(u):
        pair_copy(u, 0, True).wait_recv()
        for which in (1, 2):
            pair_copy(u, which, False).start()

    def from_second(u):
        for which in (1, 2):
            pair_copy(u, which, True).wait_recv()
        core_copy(u, False).start()

    lag = 3
    for step in range(len(units) + 2 * lag):
        chunk, turn = divmod(step, stacks - 1)
        if turn == 0 and chunk + ahead < pieces:
            both_ways([chunk + ahead], lambda copy: copy.start())
        if turn == 1 and 1 <= chunk <= matrices:
            own_copy(chunk - 1, False).start()
        if turn == 2 and chunk < members - 1:
            for j in range(swaps):
                swap_copy(j, chunk, False).start()
        for depth, stage in enumerate((from_stack, from_first, from_second)):
            if 0 <= step - lag * depth < len(units):
                stage(step - lag * depth)
    both_ways(range(pieces), lambda copy: copy.wait_send())
    for u in range(len(units)):
        passing(u, lambda copy: copy.wait_send())
        for which in range(3):
            pair_copy(u, which, False).wait_send()
        core_copy(u, False).wait_send()
        core_copy(u, True).wait_recv()
    for m in range(matrices):
        own_copy(m, False).wait_send()
        own_copy(m, True).wait_recv()
    for copy in kept:
        copy.wait()
    for j in range(swaps):
        for k in range(members - 1):
            swap_copy(j, k, False).wait_send()
            swap_copy(j, k, True).wait_recv()


def gather_kernel(matrices, swaps, members, collective_id):
    plan = []
    for index, part in enumerate(matrices):
        rows, cols = part.shape
        size = max(size for size in range(16, rows + 1, 16) if rows % size == 0 and size * cols <= 340000)
        plan += [(index, start, size, cols // 4) for start in range(0, rows, size)]
    units = len(plan) * (members // 2 - 1)
    dma = pltpu.SemaphoreType.DMA
    count = len(swaps)
    return pl.pallas_call(
        functools.partial(gather_body, members, plan, (len(matrices), count)),
        out_shape=[jax.ShapeDtypeStruct((members,) + part.shape, bf16) for part in matrices]
        + [jax.ShapeDtypeStruct(part.shape, bf16) for part in swaps],
        in_specs=in_place(len(matrices) + count),
        out_specs=in_place(len(matrices) + count),
        scratch_shapes=[
            dma((len(plan), 2)),
            dma((units,)),
            dma((units,)),
            dma((units, 3)),
            dma((units, 3)),
            dma((units,)),
            dma((units,)),
            dma((len(matrices),)),
            dma((len(matrices),)),
            dma((len(matrices) + count,)),
            dma((count, members - 1)),
            dma((count, members - 1)),
        ],
        compiler_params=pltpu.CompilerParams(collective_id=collective_id, has_side_effects=True),
        name="gather_rows",
    )(*matrices, *swaps)


def find_body(members, asked, counts, table, main_ref, tail_ref, main, tail, main_found, tail_found):
    capacity = main_ref.shape[1]
    part = capacity // 4
    step = 512

    @pl.loop(0, table.shape[1] // step)
    def _(i):
        start = pl.multiple_of(i * step, step)
        block = table[:, pl.ds(start, step)]
        main[pl.ds(start, step), :] = block[:MAIN].T
        tail[pl.ds(start, step), :] = block[MAIN:].T

    @pl.loop(0, members)
    def _(k):
        first = pl.multiple_of(k * capacity, 16)

        @pl.loop(0, (counts[k] + 7) // 8)
        def _(i):
            base = pl.multiple_of(first + i * 8, 8)
            for u in range(8):
                there = pl.ds(asked[base + u], 1)
                main_found[pl.ds(base + u, 1), :] = main[there, :]
                tail_found[pl.ds(base + u, 1), :] = tail[there, :]

        main_ref[k] = main_found[pl.ds(first, capacity), :].astype(bf16)
        pieces = [tail_found[pl.ds(first + j * part, part), :] for j in range(4)]
        tail_ref[k] = jnp.concatenate(pieces, axis=1).astype(bf16)


def find_rows(table, asked, counts, members, capacity):
    rows = table.shape[0]
    shape = jax.ShapeDtypeStruct
    smem = pl.BlockSpec(memory_space=pltpu.SMEM)
    return pl.pallas_call(
        functools.partial(find_body, members),
        out_shape=[shape((members, capacity, MAIN), bf16), shape((members, capacity // 4, MAIN), bf16)],
        in_specs=[smem, smem] + whole(1),
        out_specs=whole(2),
        scratch_shapes=[
            pltpu.VMEM((rows, MAIN), f32),
            pltpu.VMEM((rows, TAIL), f32),
            pltpu.VMEM((members * capacity, MAIN), f32),
            pltpu.VMEM((members * capacity, TAIL), f32),
        ],
        compiler_params=kernel_params(),
        name="find_rows",
    )(asked, counts, table.T)


def unpack_body(slots, main_ref, tail_ref, rows_ref, main, tail, main_row, tail_row):
    members, capacity, _ = main_ref.shape
    part = capacity // 4

    @pl.loop(0, members)
    def _(k):
        start = pl.multiple_of(k * capacity, 16)
        main[pl.ds(start, capacity), :] = main_ref[k].astype(f32)
        wide = tail_ref[k].astype(f32)
        for j in range(4):
            tail[pl.ds(start + j * part, part), :] = wide[:, j * TAIL : (j + 1) * TAIL]

    @pl.loop(0, rows_ref.shape[0] // 16)
    def _(i):
        start = pl.multiple_of(i * 16, 16)
        for u in range(16):
            slot = pl.ds(slots[start + u], 1)
            main_row[pl.ds(start + u, 1), :] = main[slot, :]
            tail_row[pl.ds(start + u, 1), :] = tail[slot, :]

    @pl.loop(0, rows_ref.shape[0] // 32)
    def _(i):
        where = pl.ds(pl.multiple_of(i * 32, 32), 32)
        rows_ref[where, :] = jnp.concatenate([main_row[where, :], tail_row[where, :]], axis=1).astype(bf16)


def unpack_rows(main, tail, slots):
    count = slots.shape[0]
    members, capacity, _ = main.shape
    return pl.pallas_call(
        unpack_body,
        out_shape=jax.ShapeDtypeStruct((count, D), bf16),
        in_specs=[pl.BlockSpec(memory_space=pltpu.SMEM)] + whole(2),
        out_specs=pl.BlockSpec(memory_space=pltpu.VMEM),
        scratch_shapes=[
            pltpu.VMEM((members * capacity, MAIN), f32),
            pltpu.VMEM((members * capacity, TAIL), f32),
            pltpu.VMEM((count, MAIN), f32),
            pltpu.VMEM((count, TAIL), f32),
        ],
        compiler_params=kernel_params(),
        name="unpack_rows",
    )(slots, main, tail)


def table_body(quarter, main_ref, tail_ref, table, first, second, table_out, first_out, second_out, tail):
    tail[...] = tail_ref[...].astype(f32).T
    start = pl.multiple_of(pl.program_id(0) // quarter * TAIL, TAIL)
    grad = jnp.concatenate([main_ref[...].astype(f32).T, tail[pl.ds(start, TAIL), :]], axis=0)
    stepped = adam_step(table[...], grad, first[...], second[...], 1.0, 0.0)
    table_out[...], first_out[...], second_out[...] = stepped


def table_step(main, tail, table, first, second):
    rows = table.shape[0]
    tile = 512
    quarter = rows // 4 // tile
    wide = pl.BlockSpec((D, tile), lambda i: (0, i))
    stepped = pl.pallas_call(
        functools.partial(table_body, quarter),
        grid=(rows // tile,),
        out_shape=[jax.ShapeDtypeStruct((D, rows), f32)] * 3,
        in_specs=[
            pl.BlockSpec((tile, MAIN), lambda i: (i, 0)),
            pl.BlockSpec((tile, MAIN), lambda i: (i % quarter, 0)),
        ]
        + [wide] * 3,
        out_specs=[wide] * 3,
        scratch_shapes=[pltpu.VMEM((MAIN, tile), f32)],
        compiler_params=kernel_params(),
        name="table_step",
    )(main, tail, table.T, first.T, second.T)
    return [part.T for part in stepped]


def place_numbers(numbers, slots, count):
    high = (slots[:, None] // 128 == jnp.arange(count // 128)[None, :]).astype(bf16)
    low = (slots[:, None] % 128 == jnp.arange(128)[None, :]).astype(bf16)
    upper, lower = (numbers // 64).astype(bf16), (numbers % 64).astype(bf16)
    placed = 64.0 * jnp.einsum("rh,rl->hl", high, low * upper[:, None], preferred_element_type=f32)
    placed += jnp.einsum("rh,rl->hl", high, low * lower[:, None], preferred_element_type=f32)
    return placed.astype(jnp.int32).reshape(-1)


def reduce_plain(grads, members):
    totals = []
    for grad in grads:
        part = lax.psum_scatter(grad, ("dp", "section"), scatter_dimension=0, tiled=True)
        totals.append(lax.all_gather(part, "section", axis=0, tiled=True))
    return totals


def per_device(
    ids,
    masks,
    labels,
    table,
    table_first,
    table_second,
    null_tokens,
    null_first,
    null_second,
    w_up,
    up_first,
    up_second,
    w_down,
    down_first,
    down_second,
    w_top,
    top_first,
    top_second,
    gains,
    gains_first,
    gains_second,
    biases,
    biases_first,
    biases_second,
    mixers,
    mixers_first,
    mixers_second,
    top_bias,
    top_bias_first,
    top_bias_second,
    head,
    head_first,
    head_second,
):
    sections = lax.axis_size("section")
    members = lax.axis_size("dp")
    section_index = lax.axis_index("section")
    micro_count = masks.shape[0]
    batch_rows = masks.shape[1]
    total = micro_count * batch_rows * members

    flat_ids = ids[0].T.reshape(-1)
    id_count = flat_ids.shape[0]
    capacity = 2 * id_count // members
    rows_dev = table.shape[0]
    owners = flat_ids // rows_dev
    local_rows = flat_ids - owners * rows_dev
    hits = (owners[:, None] == jnp.arange(members, dtype=jnp.int32)[None, :]).astype(jnp.int32)
    ranks = jnp.sum(jnp.cumsum(hits, axis=0) * hits, axis=1) - 1
    slots = owners * capacity + ranks
    requests = place_numbers(local_rows + 1, slots, members * capacity)
    asked = lax.all_to_all(
        requests.reshape(members, capacity), "dp", split_axis=0, concat_axis=0, tiled=True
    )
    asked_counts = jnp.sum((asked > 0).astype(jnp.int32), axis=1)
    asked = jnp.maximum(asked.reshape(-1) - 1, 0)
    kernels_fit = members == 8 and sections == 4
    if kernels_fit:
        main, tail = find_rows(table, asked, asked_counts, members, capacity)
        matrices = [w.astype(bf16).reshape(-1, w.shape[-1]) for w in (w_up, w_down, w_top)]
        up_copies, down_copies, top_copy, main, tail = gather_kernel(matrices, [main, tail], members, 2)
        top_copy = top_copy.reshape(-1, TOP_HID)
        looked = unpack_rows(main, tail, slots)
    else:
        found = jnp.take(table.astype(bf16), asked, axis=0, mode="clip")
        fetched = lax.all_to_all(
            found.reshape(members, capacity, D), "dp", split_axis=0, concat_axis=0, tiled=True
        ).reshape(members * capacity, D)
        looked = jnp.take(fetched, slots, axis=0, mode="clip")
        up_copies = gather_rows(w_up, section_index, sections, 1)[:, None]
        down_copies = gather_rows(w_down, section_index, sections, 1)[:, None]
        top_copy = gather_rows(w_top, section_index, sections, 0)
    looked = looked.reshape(FEATS, batch_rows, D)

    present = lax.dynamic_index_in_dim(masks, section_index, 0, keepdims=False).T > 0
    targets = lax.dynamic_index_in_dim(labels, section_index, 0, keepdims=False).astype(f32)
    state = jnp.where(present[..., None], looked, null_tokens.astype(bf16)[:, None, :])
    values = [layer_values(gains[depth], biases[depth], mixers[depth]) for depth in range(2)]
    states, kept = [], []
    for depth in range(2):
        states.append(state)
        state, *stored = layer_forward(depth, state, up_copies, down_copies, values[depth])
        kept.append(stored)
    losses, upstream, grad_top, grad_top_bias, grad_head = top_pass(
        state, top_copy, top_bias, head, targets, total
    )
    losses = losses[None, :]
    layer_grads = [None, None]
    for depth in (1, 0):
        upstream, *layer_grads[depth] = layer_backward(
            depth, upstream, states[depth], kept[depth], up_copies, down_copies, values[depth]
        )
    grad_looked = jnp.where(present[..., None], upstream, jnp.zeros_like(upstream))
    grad_null = jnp.sum(jnp.where(present[..., None], 0.0, upstream.astype(f32)), axis=1)
    input_grad = grad_looked.transpose(1, 0, 2)[None]
    smalls = (
        grad_null,
        jnp.stack([layer_grads[0][2], layer_grads[1][2]]),
        jnp.stack([layer_grads[0][3], layer_grads[1][3]]),
        jnp.stack([layer_grads[0][4], layer_grads[1][4]]),
        grad_top_bias[None, :],
        grad_head[None, :],
    )
    matrix_pairs = [pair for depth in range(2) for pair in layer_grads[depth][:2]]
    if kernels_fit:
        main, tail = pack_rows(grad_looked.reshape(id_count, D), slots, members, capacity)
        top_grad, *totals = reduce_kernel(
            [grad_top] + matrix_pairs, [], [main, tail], smalls, members, 0
        )
        matrix_grads, (main, tail), small_total = totals[:4], totals[4:6], totals[6:]
        main, tail = add_rows(main, tail, asked, asked_counts, rows_dev)
        main, tail = reduce_kernel([], [main, tail], [], [], members, 1)
        table_out = table_step(main, tail, table, table_first, table_second)
    else:
        outgoing = (
            jnp.zeros((members * capacity, D), bf16)
            .at[slots]
            .set(grad_looked.reshape(id_count, D), unique_indices=True, mode="promise_in_bounds")
        )
        arrived_rows = lax.all_to_all(
            outgoing.reshape(members, capacity, D), "dp", split_axis=0, concat_axis=0, tiled=True
        ).reshape(members * capacity, D)
        table_part = jnp.zeros((rows_dev, D), f32).at[asked].add(arrived_rows.astype(f32))
        table_sum = lax.psum_scatter(
            table_part.astype(bf16), "section", scatter_dimension=0, tiled=True
        )
        table_grad = lax.all_gather(table_sum, "section", axis=0, tiled=True).astype(f32)
        table_out = adam_step(table, table_grad, table_first, table_second, 1.0, 0.0)
        top_grad, *matrix_grads = reduce_plain(
            [nn(left, right).astype(bf16) for left, right in [grad_top] + matrix_pairs], members
        )
        small_total = lax.psum(smalls, ("section", "dp"))
    top_grad = top_grad.astype(f32)
    up_grad = jnp.stack([matrix_grads[0], matrix_grads[2]]).astype(f32)
    down_grad = jnp.stack([matrix_grads[1], matrix_grads[3]]).astype(f32)
    null_out = adam_step(null_tokens, small_total[0], null_first, null_second, 1.0, 0.0)
    up_out = adam_step(w_up, up_grad, up_first, up_second, 0.05, 0.01)
    down_out = adam_step(w_down, down_grad, down_first, down_second, 0.05, 0.01)
    top_out = adam_step(w_top, top_grad, top_first, top_second, 0.05, 0.01)
    gains_out = adam_step(gains, small_total[1], gains_first, gains_second, 1.0, 0.0)
    biases_out = adam_step(biases, small_total[2], biases_first, biases_second, 0.1, 0.0)
    mixers_out = adam_step(mixers, small_total[3], mixers_first, mixers_second, 0.2, 0.01)
    top_bias_out = adam_step(top_bias, small_total[4][0], top_bias_first, top_bias_second, 0.1, 0.0)
    head_out = adam_step(head, small_total[5][0], head_first, head_second, 0.1, 0.0)
    return (
        losses,
        input_grad,
        table_out[0],
        table_out[1],
        table_out[2],
        null_out[0],
        null_out[1],
        null_out[2],
        up_out[0],
        up_out[1],
        up_out[2],
        down_out[0],
        down_out[1],
        down_out[2],
        top_out[0],
        top_out[1],
        top_out[2],
        gains_out[0],
        gains_out[1],
        gains_out[2],
        biases_out[0],
        biases_out[1],
        biases_out[2],
        mixers_out[0],
        mixers_out[1],
        mixers_out[2],
        top_bias_out[0],
        top_bias_out[1],
        top_bias_out[2],
        head_out[0],
        head_out[1],
        head_out[2],
    )


def solution(mesh):
    placed = (
        P("section", "dp", None),
        P(None, "dp", None),
        P(None, "dp"),
        P("dp", None),
        P("dp", None),
        P("dp", None),
        P(),
        P(),
        P(),
        P(None, "dp", None),
        P(None, "dp", None),
        P(None, "dp", None),
        P(None, "dp", None),
        P(None, "dp", None),
        P(None, "dp", None),
        P("dp", None),
        P("dp", None),
        P("dp", None),
        P(),
        P(),
        P(),
        P(),
        P(),
        P(),
        P(),
        P(),
        P(),
        P(),
        P(),
        P(),
        P(),
        P(),
        P(),
    )
    return jax.shard_map(
        per_device,
        mesh=mesh,
        in_specs=placed,
        out_specs=(
            P("section", "dp"),
            P("section", "dp", None, None),
            P("dp", None),
            P("dp", None),
            P("dp", None),
            P(),
            P(),
            P(),
            P(None, "dp", None),
            P(None, "dp", None),
            P(None, "dp", None),
            P(None, "dp", None),
            P(None, "dp", None),
            P(None, "dp", None),
            P("dp", None),
            P("dp", None),
            P("dp", None),
            P(),
            P(),
            P(),
            P(),
            P(),
            P(),
            P(),
            P(),
            P(),
            P(),
            P(),
            P(),
            P(),
            P(),
            P(),
        ),
        check_vma=False,
    )
```
